128 devices in a mesh: replica: 8 (over z, x_lo), fsdp: 16 (over x_hi, y, core).
Axes of the slice: x: 4 (x_hi: 2, x_lo: 2; x = x_hi * 2 + x_lo), y: 4, z: 4, core: 2. Of those that a mesh axis runs over, the one named last changes fastest.
Arguments:
- gate_momentum: float32 [8, 1728, 4096], P('replica', 'fsdp'), may hold values from -24 to 24
- up_momentum: float32 [8, 1728, 4096], P('replica', 'fsdp'), may hold values from -24 to 24
- down_momentum: float32 [8, 320, 4096], P('replica', 'fsdp'), may hold values from -24 to 24
- gate_grad: bfloat16 [8, 1728, 4096], P('replica', 'fsdp'), may hold values from -6 to 6
- up_grad: bfloat16 [8, 1728, 4096], P('replica', 'fsdp'), may hold values from -6 to 6
- down_grad: bfloat16 [8, 320, 4096], P('replica', 'fsdp'), may hold values from -6 to 6
- gate_weight: bfloat16 [1728, 4096], P('fsdp'), may hold values from -6 to 6
- up_weight: bfloat16 [1728, 4096], P('fsdp'), may hold values from -6 to 6
- down_weight: bfloat16 [320, 4096], P('fsdp'), may hold values from -6 to 6
Outputs:
- gate_moment_next: float32 [8, 1728, 4096], P('replica', 'fsdp')
- up_moment_next: float32 [8, 1728, 4096], P('replica', 'fsdp')
- down_moment_next: float32 [8, 320, 4096], P('replica', 'fsdp')
- gate_gathered: bfloat16 [1728, 4096], replicated
- up_gathered: bfloat16 [1728, 4096], replicated
- down_gathered: bfloat16 [320, 4096], replicated
The draws below stay inside these ranges and needn't reach their ends.
All inputs are finite; a program needn't handle non-finite values.
Results may differ from the reference program's by a relative error of at most 0.001.
Values may be sent and summed in bfloat16 or wider, within the bound.
A program may use at most 192 MiB of HBM per device.

```python
import jax
import jax.numpy as jnp
from jax import lax

TILE = 64
BAND = 8
REPLICAS = 8
GATE_TILES = 1728
DOWN_TILES = 320


def steps_of(key, dims, shards, low, top_value):
    gain = 1.0
    for dim, parts in shards:
        steps = jax.random.uniform(jax.random.fold_in(jax.random.fold_in(key, 6), dim), (parts,), jnp.float32, low / len(shards), top_value / len(shards))
        gain = gain * jnp.repeat(jnp.exp(steps), dims[dim] // parts).reshape((-1,) + (1,) * (len(dims) - 1 - dim))
    return gain


def bell_draw(rng, extent, spread, bound, split=(), dtype=jnp.bfloat16):
    values = jax.random.normal(rng, extent, jnp.float32) * spread
    if len(split) > 0:
        values = steps_of(rng, extent, split, -0.22, 0.18) * values
    return jnp.clip(values, min=-bound, max=bound).astype(dtype)


def setup_inputs(seed: int = 0) -> dict:
    keys = jax.random.split(jax.random.key(seed), 10)
    return {
        "gate_momentum": bell_draw(keys[0], (REPLICAS, GATE_TILES, TILE * TILE), 4.0, 24.0, ((0, 8), (1, 16)), jnp.float32),
        "up_momentum": bell_draw(keys[1], (REPLICAS, GATE_TILES, TILE * TILE), 4.0, 24.0, ((0, 8), (1, 16)), jnp.float32),
        "down_momentum": bell_draw(keys[2], (REPLICAS, DOWN_TILES, TILE * TILE), 4.0, 24.0, ((0, 8), (1, 16)), jnp.float32),
        "gate_grad": bell_draw(keys[3], (REPLICAS, GATE_TILES, TILE * TILE), 1.0, 6.0, ((0, 8), (1, 16))),
        "up_grad": bell_draw(keys[4], (REPLICAS, GATE_TILES, TILE * TILE), 1.0, 6.0, ((0, 8), (1, 16))),
        "down_grad": bell_draw(keys[5], (REPLICAS, DOWN_TILES, TILE * TILE), 1.0, 6.0, ((0, 8), (1, 16))),
        "gate_weight": bell_draw(keys[6], (GATE_TILES, TILE * TILE), 1.0, 6.0, ((0, 16),)),
        "up_weight": bell_draw(keys[7], (GATE_TILES, TILE * TILE), 1.0, 6.0, ((0, 16),)),
        "down_weight": bell_draw(keys[8], (DOWN_TILES, TILE * TILE), 1.0, 6.0, ((0, 16),)),
    }


def band_cosines():
    freq_row = jnp.arange(BAND).astype(jnp.float32)[:, None]
    position = jnp.arange(TILE).astype(jnp.float32)[None, :]
    cosines = jnp.sqrt(2.0 / TILE) * jnp.cos(jnp.pi * (2.0 * position + 1.0) * freq_row / (2.0 * TILE))
    return jnp.where(freq_row == 0.0, cosines * jnp.sqrt(0.5), cosines)

def refresh_matrix(momentum, gradient, weight, cosines):
    highest = lax.Precision.HIGHEST
    accumulated = 0.999 * momentum + gradient.astype(jnp.float32)
    blocks = accumulated.reshape(momentum.shape[0], momentum.shape[1], TILE, TILE)
    low_band = jnp.einsum('ki,rcij,lj->rckl', cosines, blocks, cosines, precision=highest)
    removed = jnp.einsum('ki,rckl,lj->rcij', cosines, low_band, cosines, precision=highest)
    following = (blocks - removed).reshape(momentum.shape)
    averaged = lax.optimization_barrier(jnp.sum(low_band, axis=0)) / REPLICAS
    update = jnp.einsum('ki,ckl,lj->cij', cosines, averaged, cosines, precision=highest)
    update = update.reshape(weight.shape)
    root_mean = jnp.sqrt(lax.optimization_barrier(jnp.mean(update * update, axis=1, keepdims=True)) + 1e-06)
    gathered = ((1.0 - 0.5 * 0.1) * weight.astype(jnp.float32) - 0.5 * update / root_mean).astype(jnp.bfloat16)
    return (following, gathered)

def reference(gate_momentum, up_momentum, down_momentum, gate_grad, up_grad, down_grad, gate_weight, up_weight, down_weight):
    cosines = band_cosines()
    gate_next, gate_new = refresh_matrix(gate_momentum, gate_grad, gate_weight, cosines)
    up_next, up_new = refresh_matrix(up_momentum, up_grad, up_weight, cosines)
    down_next, down_new = refresh_matrix(down_momentum, down_grad, down_weight, cosines)
    return (gate_next, up_next, down_next, gate_new, up_new, down_new)
```

```python
import functools

import jax
import jax.numpy as jnp
import ml_dtypes
import numpy as np
from jax import lax
from jax.experimental import pallas as pl
from jax.experimental.pallas import tpu as pltpu
from jax.sharding import PartitionSpec as P

TILE = 64
BAND = 8
COEFS = BAND * BAND
ENTRIES = TILE * TILE
F32 = jnp.float32
BF16 = jnp.bfloat16
MESH = pl.DeviceIdType.MESH
ANY = pl.BlockSpec(memory_space=pl.ANY)
VMEM = pl.BlockSpec(memory_space=pltpu.VMEM)

ROWS = 240
BAND_ROWS = 256


def split_transform():
    freq = np.arange(BAND, dtype=np.float64)[:, None]
    position = np.arange(TILE, dtype=np.float64)[None, :]
    cosines = np.sqrt(2.0 / TILE) * np.cos(np.pi * (2.0 * position + 1.0) * freq / (2.0 * TILE))
    cosines[0] *= np.sqrt(0.5)
    product = (cosines[:, None, :, None] * cosines[None, :, None, :]).reshape(COEFS, ENTRIES)
    head = product.astype(np.float32).astype(ml_dtypes.bfloat16)
    tail = (product - head.astype(np.float64)).astype(np.float32).astype(ml_dtypes.bfloat16)
    return np.concatenate([head, head, tail, tail], axis=0)


def head_tail(value):
    head = value.astype(BF16)
    return head, (value - head.astype(F32)).astype(BF16)


def fold_kernel(
    gate_m, up_m, down_m, gate_g, up_g, down_g, gate_w, up_w, down_w, transform,
    gate_n, up_n, down_n, packed, bands, rows, lows,
):
    step = 512
    chunks = [pl.ds(at, step) for at in range(0, ENTRIES, step)]

    def place(target, gate, up, down):
        odd = lax.rem(lax.axis_index("fsdp"), 2) == 1

        @pl.when(jnp.logical_not(odd))
        def _():
            target[0:108, :] = gate
            target[108:112, :] = down[16:20]
            target[112:220, :] = up
            target[220:224, :] = jnp.zeros_like(down[0:4])
            target[224:240, :] = down[0:16]

        @pl.when(odd)
        def _():
            target[0:4, :] = down[0:4]
            target[4:112, :] = gate
            target[112:116, :] = jnp.zeros_like(down[0:4])
            target[116:224, :] = up
            target[224:240, :] = down[4:20]

    def one(momentum, gradient, following):
        total = None
        for chunk in chunks:
            accumulated = 0.999 * momentum[0, :, chunk] + gradient[0, :, chunk].astype(F32)
            following[0, :, chunk] = accumulated
            for part in head_tail(accumulated):
                product = lax.dot_general(
                    part,
                    transform[COEFS : 3 * COEFS, chunk],
                    (((1,), (1,)), ((), ())),
                    preferred_element_type=F32,
                )
                total = product if total is None else total + product
        low = total[:, :COEFS] + total[:, COEFS:]
        head, tail = head_tail(low)
        both = jnp.concatenate([head, tail], axis=1)
        twice = jnp.concatenate([both, both], axis=1)
        for chunk in chunks:
            removed = jnp.dot(twice, transform[:, chunk], preferred_element_type=F32)
            following[0, :, chunk] = following[0, :, chunk] - removed
        return both.astype(F32)

    for chunk in chunks:
        place(
            rows,
            gate_w[:, chunk].astype(F32),
            up_w[:, chunk].astype(F32),
            down_w[:, chunk].astype(F32),
        )
        packed[:, chunk] = rows[...].astype(BF16)
    gate_low = one(gate_m, gate_g, gate_n)
    up_low = one(up_m, up_g, up_n)
    down_low = one(down_m, down_g, down_n)
    place(lows, gate_low, up_low, down_low)
    lows[ROWS:BAND_ROWS, :] = jnp.zeros((BAND_ROWS - ROWS, 2 * COEFS), F32)
    bands[...] = lows[...].astype(BF16)


def fold(arrays, transform):
    like = lambda a: jax.ShapeDtypeStruct(a.shape, a.dtype)
    return pl.pallas_call(
        fold_kernel,
        name="fold",
        out_shape=(
            like(arrays[0]),
            like(arrays[1]),
            like(arrays[2]),
            jax.ShapeDtypeStruct((ROWS, ENTRIES), BF16),
            jax.ShapeDtypeStruct((BAND_ROWS, 2 * COEFS), BF16),
        ),
        in_specs=[VMEM] * 10,
        out_specs=(VMEM,) * 5,
        scratch_shapes=[pltpu.VMEM((ROWS, 512), F32), pltpu.VMEM((BAND_ROWS, 2 * COEFS), F32)],
        compiler_params=pltpu.CompilerParams(vmem_limit_bytes=28 * 2**20),
    )(*arrays, transform)


UNIT_US, HOP_US, BANDS_US = 2.85, 1.0, 9.0
SIZE = {"E": 1.0, "D": 1.0, "H": 0.5, "C": 0.25}


def plan_messages():
    out = []
    band = lambda q: [("E", 0, q)] + [("D", q, k) for k in range(3)] + [("H", q), ("C", q)]
    for link, near in (("ym", 3), ("yp", 1)):
        for unit in band(0) + band(1) + [("E", dz, 1) for dz in (1, 2, 3)]:
            out.append((link, (0, near, unit), (0, 0, unit), None))
    for link, near, q, dz, half in (("ym", 3, 0, 1, 0), ("yp", 1, 1, 3, 1)):
        for unit in band(q) + [("E", dz, 1)]:
            out.append((link, (0, 2, unit), (0, near, unit), None))
        out.append((link, (0, 2, ("E", 2, 1)), (0, near, ("E", 2, 1)), half))
    for dy in range(4):
        for own, other in zip(band(0), band(1)):
            out.append(("xc", (1, dy, own), (0, dy, other), None))
            out.append(("xi", (1, dy, other), (1, dy, own), None))
    for link, dz, q, half in (("zm", 3, 0, 0), ("zp", 1, 1, 1)):
        for dy in (1, 2, 3):
            out.append((link, (0, dy, ("E", dz, 0)), (0, dy, ("E", 0, 0)), None))
            out.append((link, (0, dy, ("E", 2, 0)), (0, dy, ("E", dz, 0)), half))
        for dy in range(4):
            for each in (0, 1):
                out.append((link, (1, dy, ("E", dz, each)), (1, dy, ("E", 0, each)), None))
            out.append((link, (1, dy, ("E", 2, q)), (1, dy, ("E", dz, q)), None))
    return out


def plan():
    messages = plan_messages()
    users = {}
    for index, message in enumerate(messages):
        users.setdefault(message[2], []).append(index)
    cost = [SIZE[m[1][2][0]] * (0.5 if m[3] is not None else 1.0) * UNIT_US for m in messages]
    known = {}

    def tail(index):
        if index not in known:
            after = [tail(user) for user in users.get(messages[index][1], [])]
            known[index] = cost[index] + HOP_US + max(after + [0.0])
        return known[index]

    here = {}
    for message in messages:
        if message[2][:2] == (0, 0):
            here[message[2]] = BANDS_US if message[2][2][0] == "C" else 0.0
    free = dict.fromkeys(("ym", "yp", "xc", "xi", "zm", "zp"), 0.0)
    left = list(range(len(messages)))
    events = [(BANDS_US - 0.5, 0, -1)]
    while left:
        best = None
        for link in free:
            ready = [
                (max(free[link], here[messages[i][2]]), -tail(i), i)
                for i in left
                if messages[i][0] == link and messages[i][2] in here
            ]
            if ready:
                first = min(ready)[0]
                pick = min((r for r in ready if r[0] <= first), key=lambda r: r[1:])
                if best is None or pick[0] < best[0]:
                    best = (pick[0], link, pick[2])
        begin, link, index = best
        left.remove(index)
        free[link] = begin + cost[index]
        key = messages[index][1]
        arrive = free[link] + HOP_US
        events.append((max(here[messages[index][2]] + 0.01, begin - 1.2 * UNIT_US), 1, index))
        events.append((arrive, 0, index))
        here[key] = max(here.get(key, 0.0), arrive)
    return messages, sorted(events)


def spread_kernel(
    packed, bands, landing, coefs,
    peers, mine, received, own, band_sent, band_received, sent, sent_c, side_sent, side_sent_c,
    side_received, side_received_c,
):
    replica, shard = lax.axis_index("replica"), lax.axis_index("fsdp")
    z, lo = lax.div(replica, 2), lax.rem(replica, 2)
    hi, y, core = lax.div(shard, 8), lax.rem(lax.div(shard, 2), 4), lax.rem(shard, 2)
    device = lambda z, lo, hi, y, core: (2 * z + lo, 8 * hi + 2 * y + core)
    turn = lambda at, by: lax.rem(at + by, 4)
    target = {
        "ym": device(z, lo, hi, turn(y, 1), core),
        "yp": device(z, lo, hi, turn(y, 3), core),
        "xc": device(z, 1 - lo, 1 - hi, y, core),
        "xi": device(z, 1 - lo, hi, y, core),
        "zm": device(turn(z, 1), lo, hi, y, core),
        "zp": device(turn(z, 3), lo, hi, y, core),
    }
    sibling = device(z, lo, hi, y, 1 - core)
    fellows = [
        device(turn(z, dz), lo if same else 1 - lo, hi, y, core)
        for dz in range(4)
        for same in (True, False)
        if not (dz == 0 and same)
    ]

    barrier = pltpu.get_barrier_semaphore()
    partners = [target["ym"], target["yp"], target["xc"], sibling] + fellows
    for partner in partners:
        pl.semaphore_signal(barrier, 1, device_id=partner, device_id_type=MESH)
    pl.semaphore_wait(barrier, len(partners))

    def remote(source, dest, send, receive, to):
        return pltpu.make_async_remote_copy(
            src_ref=source, dst_ref=dest, send_sem=send, recv_sem=receive, device_id=to, device_id_type=MESH
        )

    block_at = {
        (dx, dy): 8 * (hi if dx == 0 else 1 - hi) + 2 * turn(y, dy) + core for dx in range(2) for dy in range(4)
    }
    parity = (lo, 1 - lo)

    def place(array_rows, key, half):
        kind = key[0]
        columns = slice(None) if half is None else pl.ds(half * (ENTRIES // 2), ENTRIES // 2)
        if kind == "E":
            start = 32 * turn(z, key[1]) + 16 * parity[key[2]]
        elif kind == "D":
            start = 128 + 48 * parity[key[1]] + 16 * key[2]
        elif kind == "H":
            start = 224
            columns = pl.ds(pl.multiple_of((ENTRIES // 2) * parity[key[1]], 128), ENTRIES // 2)
        else:
            return pl.ds(pl.multiple_of(128 * parity[key[1]], 16), 128), slice(None)
        return (pl.ds(start if isinstance(start, int) else pl.multiple_of(start, 16), 16), columns)

    def refs(key, half):
        dx, dy, unit = key
        rows, columns = place(None, unit, half)
        block = block_at[(dx, dy)]
        if unit[0] == "C":
            here = coefs.at[block, rows, columns]
            return (mine.at[rows, columns] if (dx, dy) == (0, 0) else here), here
        here = landing.at[block, rows, columns]
        return (packed.at[rows, columns] if (dx, dy) == (0, 0) else here), here

    for fellow in fellows:
        remote(bands, peers.at[replica], band_sent, band_received, fellow).start()

    messages, events = plan()
    me = block_at[(0, 0)]
    own_copy = pltpu.make_async_copy(packed, landing.at[me], own.at[0])
    own_coefs = pltpu.make_async_copy(mine, coefs.at[me], own.at[1])

    def send(index):
        link, key, key_there, half = messages[index]
        source, dest = refs(key_there, half)
        is_coefs = key[2][0] == "C"
        remote(source, dest, sent_c if is_coefs else sent, received.at[index], target[link]).start()

    def take(index):
        link, key, _, half = messages[index]
        _, dest = refs(key, half)
        is_coefs = key[2][0] == "C"
        remote(dest, dest, sent_c if is_coefs else sent, received.at[index], target[link]).wait_recv()
        remote(
            dest,
            dest,
            side_sent_c if is_coefs else side_sent,
            side_received_c if is_coefs else side_received,
            sibling,
        ).start()

    def average():
        peers[replica] = bands[...]
        remote(peers.at[0:7], peers.at[0:7], band_sent, band_received, sibling).wait_recv()
        total = peers[0].astype(F32)
        for each in range(1, 8):
            total = total + peers[each].astype(F32)
        averaged = (total[:, :COEFS] + total[:, COEFS:]) / 8.0
        square = jnp.sum(averaged * averaged, axis=1, keepdims=True) / ENTRIES
        head, tail = head_tail(-0.5 * averaged / jnp.sqrt(square + 1e-06))
        mine[...] = jnp.concatenate([head, tail], axis=1)
        own_coefs.start()
        remote(mine, coefs.at[me], side_sent_c, side_received_c, sibling).start()

    first = True
    for when, kind, index in events:
        if index >= 0 and kind == 1:
            send(index)
            continue
        if first:
            own_copy.start()
            remote(packed, landing.at[me], side_sent, side_received, sibling).start()
            first = False
        if index < 0:
            average()
        else:
            take(index)

    own_copy.wait()
    own_coefs.wait()
    remote(peers.at[0:7], peers.at[0:7], band_sent, band_received, sibling).wait_send()
    remote(landing.at[0:7], landing.at[0:7], sent, side_received, sibling).wait_send()
    remote(coefs.at[0:7], coefs.at[0:7], sent_c, side_received_c, sibling).wait_send()
    last = remote(landing.at[0:8], landing.at[0:8], side_sent, side_received, sibling)
    last_c = remote(coefs.at[0:8], coefs.at[0:8], side_sent_c, side_received_c, sibling)
    last.wait_send()
    last_c.wait_send()
    last.wait_recv()
    last_c.wait_recv()


def spread(packed, bands):
    dma = pltpu.SemaphoreType.DMA
    return pl.pallas_call(
        spread_kernel,
        name="spread",
        out_shape=(
            jax.ShapeDtypeStruct((16, ROWS, ENTRIES), BF16),
            jax.ShapeDtypeStruct((16, BAND_ROWS, 2 * COEFS), BF16),
        ),
        in_specs=[ANY, VMEM],
        out_specs=(ANY, ANY),
        scratch_shapes=[
            pltpu.VMEM((8, BAND_ROWS, 2 * COEFS), BF16),
            pltpu.VMEM((BAND_ROWS, 2 * COEFS), BF16),
            dma((len(plan_messages()),)),
            dma((2,)),
        ]
        + [dma] * 8,
        compiler_params=pltpu.CompilerParams(
            collective_id=0, has_side_effects=True, vmem_limit_bytes=8 * 2**20
        ),
    )(packed, bands)


QUAD = 4
WIDTH = 1024


def refresh_kernel(landing, coefs, transform, gate, up, down):
    low_half = lax.broadcasted_iota(jnp.int32, (8, 256), 0) < 4
    for at in range(0, WIDTH, 256):
        chunk = pl.ds(at, 256)
        gates, ups, downs = [], [], []

        def renewed(each):
            both = coefs[each, 0:ROWS, :]
            twice = jnp.concatenate([both, both], axis=1)
            update = jnp.dot(twice, transform[:, chunk], preferred_element_type=F32)
            return (1.0 - 0.5 * 0.1) * landing[each, :, chunk].astype(F32) + update

        for pair in range(QUAD // 2):
            even, odd = renewed(2 * pair), renewed(2 * pair + 1)
            join = lambda a, b: jnp.where(low_half, a, b)
            gates += [even[0:104], join(even[104:112], odd[0:8]), odd[8:112]]
            ups += [even[112:216], join(even[216:224], odd[112:120]), odd[120:224]]
            downs += [
                even[224:240],
                join(pltpu.roll(even[104:112], 4, 0), pltpu.roll(odd[0:8], 4, 0)),
                odd[224:240],
            ]
        gate[:, chunk] = jnp.concatenate(gates, axis=0).astype(BF16)
        up[:, chunk] = jnp.concatenate(ups, axis=0).astype(BF16)
        down[:, chunk] = jnp.concatenate(downs, axis=0).astype(BF16)


def refresh(landing, coefs, transform):
    whole = lambda rows: jax.ShapeDtypeStruct((16 * rows, ENTRIES), BF16)
    out = lambda rows: pl.BlockSpec((QUAD * rows, WIDTH), lambda g, c: (g, c))
    return pl.pallas_call(
        refresh_kernel,
        name="refresh",
        grid=(16 // QUAD, ENTRIES // WIDTH),
        out_shape=(whole(108), whole(108), whole(20)),
        in_specs=[
            pl.BlockSpec((QUAD, ROWS, WIDTH), lambda g, c: (g, 0, c)),
            pl.BlockSpec((QUAD, BAND_ROWS, 2 * COEFS), lambda g, c: (g, 0, 0)),
            pl.BlockSpec((4 * COEFS, WIDTH), lambda g, c: (0, c)),
        ],
        out_specs=(out(108), out(108), out(20)),
        compiler_params=pltpu.CompilerParams(vmem_limit_bytes=20 * 2**20),
    )(landing, coefs, transform)


def on_device(*arrays):
    transform = jnp.asarray(split_transform())
    gate_next, up_next, down_next, packed, bands = fold(arrays, transform)
    landing, coefs = spread(packed, bands)
    gate_whole, up_whole, down_whole = refresh(landing, coefs, transform)
    return (gate_next, up_next, down_next, gate_whole, up_whole, down_whole)


def solution(mesh):
    by_replica, by_shard = P("replica", "fsdp", None), P("fsdp", None)
    return jax.shard_map(
        on_device,
        mesh=mesh,
        in_specs=(by_replica,) * 6 + (by_shard,) * 3,
        out_specs=(by_replica,) * 3 + (P(),) * 3,
        check_vma=False,
    )
```

```python
import functools

import jax
import jax.numpy as jnp
import ml_dtypes
import numpy as np
from jax import lax
from jax.experimental import pallas as pl
from jax.experimental.pallas import tpu as pltpu
from jax.sharding import PartitionSpec as P

TILE = 64
BAND = 8
COEFS = BAND * BAND
ENTRIES = TILE * TILE
F32 = jnp.float32
BF16 = jnp.bfloat16
MESH = pl.DeviceIdType.MESH
ANY = pl.BlockSpec(memory_space=pl.ANY)
VMEM = pl.BlockSpec(memory_space=pltpu.VMEM)

ROWS = 240
BAND_ROWS = 256
EARLY = 128
STEP = 512


def split_transform():
    freq = np.arange(BAND, dtype=np.float64)[:, None]
    position = np.arange(TILE, dtype=np.float64)[None, :]
    cosines = np.sqrt(2.0 / TILE) * np.cos(np.pi * (2.0 * position + 1.0) * freq / (2.0 * TILE))
    cosines[0] *= np.sqrt(0.5)
    product = (cosines[:, None, :, None] * cosines[None, :, None, :]).reshape(COEFS, ENTRIES)
    head = product.astype(np.float32).astype(ml_dtypes.bfloat16)
    tail = (product - head.astype(np.float64)).astype(np.float32).astype(ml_dtypes.bfloat16)
    return np.concatenate([head, head, tail, tail], axis=0)


def in_hbm(*arrays):
    return tuple(pltpu.with_memory_space_constraint(a, pltpu.HBM) for a in arrays)


def head_tail(value):
    head = value.astype(BF16)
    return head, (value - head.astype(F32)).astype(BF16)


UNIT_US, HOP_US, BANDS_US = 2.85, 3.0, 22.0
FOLD_US, REMOVE_US = 14.0, 24.0
SIZE = {"E": 1.0, "D": 1.0, "H": 0.5, "C": 0.25}


def plan_messages():
    out = []
    band = lambda q: [("E", 0, q)] + [("D", q, k) for k in range(3)] + [("H", q), ("C", q)]
    for link, near in (("ym", 3), ("yp", 1)):
        for unit in band(0) + band(1) + [("E", dz, 1) for dz in (1, 2, 3)]:
            out.append((link, (0, near, unit), (0, 0, unit), None))
    for link, near, q, dz, half in (("ym", 3, 0, 1, 0), ("yp", 1, 1, 3, 1)):
        for unit in band(q) + [("E", dz, 1)]:
            out.append((link, (0, 2, unit), (0, near, unit), None))
        out.append((link, (0, 2, ("E", 2, 1)), (0, near, ("E", 2, 1)), half))
    for dy in range(4):
        for own, other in zip(band(0), band(1)):
            out.append(("xc", (1, dy, own), (0, dy, other), None))
            out.append(("xi", (1, dy, other), (1, dy, own), None))
    for link, dz, q, half in (("zm", 3, 0, 0), ("zp", 1, 1, 1)):
        for dy in (1, 2, 3):
            out.append((link, (0, dy, ("E", dz, 0)), (0, dy, ("E", 0, 0)), None))
            out.append((link, (0, dy, ("E", 2, 0)), (0, dy, ("E", dz, 0)), half))
        for dy in range(4):
            for each in (0, 1):
                out.append((link, (1, dy, ("E", dz, each)), (1, dy, ("E", 0, each)), None))
            out.append((link, (1, dy, ("E", 2, q)), (1, dy, ("E", dz, q)), None))
    return out


def plan():
    messages = plan_messages()
    users = {}
    for index, message in enumerate(messages):
        users.setdefault(message[2], []).append(index)
    cost = [SIZE[m[1][2][0]] * (0.5 if m[3] is not None else 1.0) * UNIT_US for m in messages]
    known = {}

    def tail(index):
        if index not in known:
            after = [tail(user) for user in users.get(messages[index][1], [])]
            known[index] = cost[index] + HOP_US + max(after + [0.0])
        return known[index]

    here = {}
    for message in messages:
        if message[2][:2] == (0, 0):
            here[message[2]] = BANDS_US if message[2][2][0] == "C" else 0.0
    free = dict.fromkeys(("ym", "yp", "xc", "xi", "zm", "zp"), 0.0)
    left = list(range(len(messages)))
    steps = 3 * (ENTRIES // STEP)
    events = [(FOLD_US * (i + 0.5) / steps, 2, i) for i in range(steps)]
    events += [(FOLD_US + 0.1, 2, steps), (BANDS_US - 0.5, 2, steps + 1)]
    events += [(REMOVE_US + FOLD_US * (i + 0.5) / steps, 2, steps + 2 + i) for i in range(steps)]
    while left:
        best = None
        for link in free:
            ready = [
                (max(free[link], here[messages[i][2]]), -tail(i), i)
                for i in left
                if messages[i][0] == link and messages[i][2] in here
            ]
            if ready:
                first = min(ready)[0]
                pick = min((r for r in ready if r[0] <= first), key=lambda r: r[1:])
                if best is None or pick[0] < best[0]:
                    best = (pick[0], link, pick[2])
        begin, link, index = best
        left.remove(index)
        free[link] = begin + cost[index]
        key = messages[index][1]
        arrive = free[link] + HOP_US
        events.append((max(here[messages[index][2]] + 0.01, begin - 0.9 * UNIT_US), 1, index))
        events.append((arrive, 0, index))
        here[key] = max(here.get(key, 0.0), arrive)
    return messages, sorted(events)


def spread_kernel(
    gate_m, up_m, down_m, gate_g, up_g, down_g, gate_w, up_w, down_w, transform_in,
    gate_n, up_n, down_n, early, late, coefs,
    m0, m1, m2, g0, g1, g2, w0, w1, w2, transform, packed, rows, totals, lows, bands,
    peers, mine, loaded, stored, received, own, band_sent, band_received, sent, sent_c, side_sent, side_sent_c,
    side_received, side_received_c,
):
    loads = [
        pltpu.make_async_copy(a, b, loaded.at[i])
        for i, (a, b) in enumerate(
            zip(
                (gate_w, up_w, down_w, gate_m, up_m, down_m, gate_g, up_g, down_g, transform_in),
                (w0, w1, w2, m0, m1, m2, g0, g1, g2, transform),
            )
        )
    ]
    for load in loads:
        load.start()
    stores = [
        pltpu.make_async_copy(a, b, stored.at[i])
        for i, (a, b) in enumerate(((m0, gate_n), (m1, up_n), (m2, down_n)))
    ]
    replica, shard = lax.axis_index("replica"), lax.axis_index("fsdp")
    z, lo = lax.div(replica, 2), lax.rem(replica, 2)
    hi, y, core = lax.div(shard, 8), lax.rem(lax.div(shard, 2), 4), lax.rem(shard, 2)
    device = lambda z, lo, hi, y, core: (2 * z + lo, 8 * hi + 2 * y + core)
    turn = lambda at, by: lax.rem(at + by, 4)
    target = {
        "ym": device(z, lo, hi, turn(y, 1), core),
        "yp": device(z, lo, hi, turn(y, 3), core),
        "xc": device(z, 1 - lo, 1 - hi, y, core),
        "xi": device(z, 1 - lo, hi, y, core),
        "zm": device(turn(z, 1), lo, hi, y, core),
        "zp": device(turn(z, 3), lo, hi, y, core),
    }
    sibling = device(z, lo, hi, y, 1 - core)
    fellows = [
        device(turn(z, dz), lo if same else 1 - lo, hi, y, core)
        for dz in range(4)
        for same in (True, False)
        if not (dz == 0 and same)
    ]

    barrier = pltpu.get_barrier_semaphore()
    partners = [target["ym"], target["yp"], target["xc"], sibling] + fellows
    for partner in partners:
        pl.semaphore_signal(barrier, 1, device_id=partner, device_id_type=MESH)

    chunks = [pl.ds(at, STEP) for at in range(0, ENTRIES, STEP)]

    def lay(block, gate, up, down):
        @pl.when(core == 0)
        def _():
            block[0:108, :] = gate
            block[108:112, :] = down[16:20]
            block[112:220, :] = up
            block[220:224, :] = jnp.zeros_like(down[0:4])
            block[224:240, :] = down[0:16]

        @pl.when(core == 1)
        def _():
            block[0:4, :] = down[0:4]
            block[4:112, :] = gate
            block[112:116, :] = jnp.zeros_like(down[0:4])
            block[116:224, :] = up
            block[224:240, :] = down[4:20]

    for load in loads[:3]:
        load.wait()
    for chunk in chunks:
        lay(rows, *(w[:, chunk].astype(F32) for w in (w0, w1, w2)))
        packed[:, chunk] = rows[...].astype(BF16)
    pl.semaphore_wait(barrier, len(partners))

    groups = ENTRIES // 128
    windows = ((m0, g0, 0, 108), (m1, g1, 112, 108), (m2, g2, 224, 20))

    def accumulate(window, chunk):
        momentum, gradient, at, tiles = windows[window]
        if chunk == 0:
            loads[3 + window].wait()
            loads[6 + window].wait()
            if window == 0:
                loads[9].wait()
        pieces = []
        for group in range(chunk * STEP // 128, (chunk + 1) * STEP // 128):
            line = pl.ds(group, tiles, stride=groups)
            piece = 0.999 * momentum[line, :] + gradient[0, :, pl.ds(128 * group, 128)].astype(F32)
            momentum[line, :] = piece
            pieces.append(piece)
        total = None
        for part in head_tail(jnp.concatenate(pieces, axis=1)):
            product = lax.dot_general(
                part,
                transform[COEFS : 3 * COEFS, chunks[chunk]],
                (((1,), (1,)), ((), ())),
                preferred_element_type=F32,
            )
            total = product if total is None else total + product
        spot = pl.ds(at, tiles)
        totals[spot, :] = total if chunk == 0 else totals[spot, :] + total

    def finish_bands():
        both = []
        for _, _, at, tiles in windows:
            total = totals[pl.ds(at, tiles), :]
            both.append(jnp.concatenate(head_tail(total[:, :COEFS] + total[:, COEFS:]), axis=1).astype(F32))
            totals[pl.ds(at, tiles), :] = both[-1]
        lay(lows, *both)
        lows[ROWS:BAND_ROWS, :] = jnp.zeros((BAND_ROWS - ROWS, 2 * COEFS), F32)
        bands[...] = lows[...].astype(BF16)
        for fellow in fellows:
            remote(bands, peers.at[replica], band_sent, band_received, fellow).start()

    def remove(window, chunk):
        momentum, _, at, tiles = windows[window]
        both = totals[pl.ds(at, tiles), :].astype(BF16)
        twice = jnp.concatenate([both, both], axis=1)
        removed = jnp.dot(twice, transform[:, chunks[chunk]], preferred_element_type=F32)
        for part in range(STEP // 128):
            line = pl.ds(chunk * STEP // 128 + part, tiles, stride=groups)
            momentum[line, :] = momentum[line, :] - removed[:, 128 * part : 128 * (part + 1)]
        if chunk == len(chunks) - 1:
            stores[window].start()

    def remote(source, dest, send, receive, to):
        return pltpu.make_async_remote_copy(
            src_ref=source, dst_ref=dest, send_sem=send, recv_sem=receive, device_id=to, device_id_type=MESH
        )

    block_at = {
        (dx, dy): 8 * (hi if dx == 0 else 1 - hi) + 2 * turn(y, dy) + core for dx in range(2) for dy in range(4)
    }
    parity = (lo, 1 - lo)

    def place(array_rows, key, half):
        kind = key[0]
        columns = slice(None) if half is None else pl.ds(half * (ENTRIES // 2), ENTRIES // 2)
        if kind == "E":
            start = 32 * turn(z, key[1]) + 16 * parity[key[2]]
        elif kind == "D":
            start = EARLY + 48 * parity[key[1]] + 16 * key[2]
        elif kind == "H":
            start = 224
            columns = pl.ds(pl.multiple_of((ENTRIES // 2) * parity[key[1]], 128), ENTRIES // 2)
        else:
            return pl.ds(pl.multiple_of(128 * parity[key[1]], 16), 128), slice(None)
        return (pl.ds(start if isinstance(start, int) else pl.multiple_of(start, 16), 16), columns)

    part = lambda unit: early if unit[0] == "E" else late
    rows_in = lambda unit, rows: rows if unit[0] == "E" else pl.ds(rows.start - EARLY, rows.size)

    def refs(key, half):
        dx, dy, unit = key
        rows, columns = place(None, unit, half)
        block = block_at[(dx, dy)]
        if unit[0] == "C":
            here = coefs.at[block, rows, columns]
            return (mine.at[rows, columns] if (dx, dy) == (0, 0) else here), here
        if (dx, dy) == (0, 0):
            return packed.at[rows, columns], part(unit).at[block, rows_in(unit, rows), columns]
        here = part(unit).at[block, rows_in(unit, rows), columns]
        return here, here

    messages, events = plan()
    slices = [functools.partial(accumulate, w, c) for w in range(3) for c in range(len(chunks))]
    slices += [finish_bands, lambda: average()]
    slices += [functools.partial(remove, w, c) for w in range(3) for c in range(len(chunks))]
    me = block_at[(0, 0)]
    halves = ((packed.at[0:EARLY], early.at[me]), (packed.at[EARLY:ROWS], late.at[me]))
    own_copies = [pltpu.make_async_copy(a, b, own.at[i]) for i, (a, b) in enumerate(halves)]
    own_coefs = pltpu.make_async_copy(mine, coefs.at[me], own.at[2])

    def send(index):
        link, key, key_there, half = messages[index]
        source, dest = refs(key_there, half)
        is_coefs = key[2][0] == "C"
        which = sent_c if is_coefs else sent.at[int(key[2][0] != "E")]
        remote(source, dest, which, received.at[index], target[link]).start()

    def take(index):
        link, key, _, columns = messages[index]
        _, dest = refs(key, columns)
        is_coefs = key[2][0] == "C"
        remote(dest, dest, sent_c, received.at[index], target[link]).wait_recv()
        half = int(key[2][0] != "E")
        remote(
            dest,
            dest,
            side_sent_c if is_coefs else side_sent.at[half],
            side_received_c if is_coefs else side_received.at[half],
            sibling,
        ).start()

    def average():
        peers[replica] = bands[...]
        remote(peers.at[0:7], peers.at[0:7], band_sent, band_received, sibling).wait_recv()
        total = peers[0].astype(F32)
        for each in range(1, 8):
            total = total + peers[each].astype(F32)
        averaged = (total[:, :COEFS] + total[:, COEFS:]) / 8.0
        square = jnp.sum(averaged * averaged, axis=1, keepdims=True) / ENTRIES
        head, tail = head_tail(-0.5 * averaged / jnp.sqrt(square + 1e-06))
        mine[...] = jnp.concatenate([head, tail], axis=1)
        own_coefs.start()
        remote(mine, coefs.at[me], side_sent_c, side_received_c, sibling).start()

    first = True
    for when, kind, index in events:
        if kind == 1:
            send(index)
            continue
        if first:
            for copy in own_copies:
                copy.start()
            for i, (source, dest) in enumerate(halves):
                remote(source, dest, side_sent.at[i], side_received.at[i], sibling).start()
            first = False
        if kind == 2:
            slices[index]()
        else:
            take(index)

    for copy in own_copies:
        copy.wait()
    own_coefs.wait()
    for store in stores:
        store.wait()
    remote(peers.at[0:7], peers.at[0:7], band_sent, band_received, sibling).wait_send()
    for i, each in enumerate((early, late)):
        remote(each.at[0:7], each.at[0:7], sent.at[i], side_received.at[i], sibling).wait_send()
    remote(coefs.at[0:7], coefs.at[0:7], sent_c, side_received_c, sibling).wait_send()
    for i, each in enumerate((early, late)):
        remote(each.at[0:8], each.at[0:8], side_sent.at[i], side_received.at[i], sibling).wait()
    remote(coefs.at[0:8], coefs.at[0:8], side_sent_c, side_received_c, sibling).wait()


def spread(arrays, transform):
    dma = pltpu.SemaphoreType.DMA
    lines = [a.reshape(-1, 128) for a in arrays[:3]]
    here = lambda a: pltpu.VMEM(a.shape, a.dtype)
    band = pltpu.VMEM((BAND_ROWS, 2 * COEFS), BF16)
    return pl.pallas_call(
        spread_kernel,
        name="spread",
        out_shape=tuple(jax.ShapeDtypeStruct(a.shape, F32) for a in lines)
        + (
            jax.ShapeDtypeStruct((16, EARLY, ENTRIES), BF16),
            jax.ShapeDtypeStruct((16, ROWS - EARLY, ENTRIES), BF16),
            jax.ShapeDtypeStruct((16, BAND_ROWS, 2 * COEFS), BF16),
        ),
        in_specs=[ANY] * 10,
        out_specs=(ANY,) * 6,
        scratch_shapes=[here(a) for a in (*lines, *arrays[3:], transform)]
        + [
            pltpu.VMEM((ROWS, ENTRIES), BF16),
            pltpu.VMEM((ROWS, STEP), F32),
            pltpu.VMEM((BAND_ROWS, 2 * COEFS), F32),
            pltpu.VMEM((BAND_ROWS, 2 * COEFS), F32),
            band,
            pltpu.VMEM((8, BAND_ROWS, 2 * COEFS), BF16),
            band,
            dma((10,)),
            dma((3,)),
            dma((len(plan_messages()),)),
            dma((3,)),
        ]
        + [dma] * 2
        + [dma((2,)), dma, dma((2,)), dma, dma((2,)), dma],
        compiler_params=pltpu.CompilerParams(
            collective_id=0, has_side_effects=True, vmem_limit_bytes=16 * 2**20
        ),
    )(*in_hbm(*lines, *arrays[3:], transform))


QUAD = 4
WIDTH = 1024


def refresh_kernel(
    early, late, coefs, transform, gate_m, up_m, down_m, gate, up, down, gate_n, up_n, down_n
):
    gate_n[...] = gate_m[...]
    up_n[...] = up_m[...]
    down_n[...] = down_m[...]
    low_half = lax.broadcasted_iota(jnp.int32, (8, 256), 0) < 4
    for at in range(0, WIDTH, 256):
        chunk = pl.ds(at, 256)
        gates, ups, downs = [], [], []

        def renewed(each):
            both = coefs[each, 0:ROWS, :]
            twice = jnp.concatenate([both, both], axis=1)
            update = jnp.dot(twice, transform[:, chunk], preferred_element_type=F32)
            return (1.0 - 0.5 * 0.1) * jnp.concatenate(
                [early[each, :, chunk].astype(F32), late[each, :, chunk].astype(F32)], axis=0
            ) + update

        for pair in range(QUAD // 2):
            even, odd = renewed(2 * pair), renewed(2 * pair + 1)
            join = lambda a, b: jnp.where(low_half, a, b)
            gates += [even[0:104], join(even[104:112], odd[0:8]), odd[8:112]]
            ups += [even[112:216], join(even[216:224], odd[112:120]), odd[120:224]]
            downs += [
                even[224:240],
                join(pltpu.roll(even[104:112], 4, 0), pltpu.roll(odd[0:8], 4, 0)),
                odd[224:240],
            ]
        gate[:, chunk] = jnp.concatenate(gates, axis=0).astype(BF16)
        up[:, chunk] = jnp.concatenate(ups, axis=0).astype(BF16)
        down[:, chunk] = jnp.concatenate(downs, axis=0).astype(BF16)


def refresh(early, late, coefs, transform, moments):
    whole = lambda rows: jax.ShapeDtypeStruct((16 * rows, ENTRIES), BF16)
    out = lambda rows: pl.BlockSpec((QUAD * rows, WIDTH), lambda g, c: (g, c))
    steps = (16 // QUAD) * (ENTRIES // WIDTH)
    moment_specs = tuple(
        pl.BlockSpec((a.shape[0] // steps, 128), lambda g, c: (g * (ENTRIES // WIDTH) + c, 0)) for a in moments
    )
    return pl.pallas_call(
        refresh_kernel,
        name="refresh",
        grid=(16 // QUAD, ENTRIES // WIDTH),
        out_shape=(whole(108), whole(108), whole(20))
        + tuple(jax.ShapeDtypeStruct(a.shape, F32) for a in moments),
        in_specs=[
            pl.BlockSpec((QUAD, EARLY, WIDTH), lambda g, c: (g, 0, c)),
            pl.BlockSpec((QUAD, ROWS - EARLY, WIDTH), lambda g, c: (g, 0, c)),
            pl.BlockSpec((QUAD, BAND_ROWS, 2 * COEFS), lambda g, c: (g, 0, 0)),
            pl.BlockSpec((4 * COEFS, WIDTH), lambda g, c: (0, c)),
            *moment_specs,
        ],
        out_specs=(out(108), out(108), out(20)) + moment_specs,
        compiler_params=pltpu.CompilerParams(vmem_limit_bytes=14 * 2**20),
    )(early, late, coefs, transform, *moments)


def on_device(*arrays):
    transform = jnp.asarray(split_transform())
    *moments, early, late, coefs = spread(arrays, transform)
    *whole, gate_next, up_next, down_next = refresh(early, late, coefs, transform, moments)
    following = [a.reshape(b.shape) for a, b in zip((gate_next, up_next, down_next), arrays)]
    return (*following, *whole)


def solution(mesh):
    by_replica, by_shard = P("replica", "fsdp", None), P("fsdp", None)
    return jax.shard_map(
        on_device,
        mesh=mesh,
        in_specs=(by_replica,) * 6 + (by_shard,) * 3,
        out_specs=(by_replica,) * 3 + (P(),) * 3,
        check_vma=False,
    )
```

```python
import functools

import jax
import jax.numpy as jnp
import ml_dtypes
import numpy as np
from jax import lax
from jax.experimental import pallas as pl
from jax.experimental.pallas import tpu as pltpu
from jax.sharding import PartitionSpec as P

TILE = 64
BAND = 8
COEFS = BAND * BAND
ENTRIES = TILE * TILE
F32 = jnp.float32
BF16 = jnp.bfloat16
MESH = pl.DeviceIdType.MESH
ANY = pl.BlockSpec(memory_space=pl.ANY)
VMEM = pl.BlockSpec(memory_space=pltpu.VMEM)

ROWS = 240
BAND_ROWS = 256
EARLY = 128
STEP = 512


def split_transform():
    freq = np.arange(BAND, dtype=np.float64)[:, None]
    position = np.arange(TILE, dtype=np.float64)[None, :]
    cosines = np.sqrt(2.0 / TILE) * np.cos(np.pi * (2.0 * position + 1.0) * freq / (2.0 * TILE))
    cosines[0] *= np.sqrt(0.5)
    product = (cosines[:, None, :, None] * cosines[None, :, None, :]).reshape(COEFS, ENTRIES)
    head = product.astype(np.float32).astype(ml_dtypes.bfloat16)
    tail = (product - head.astype(np.float64)).astype(np.float32).astype(ml_dtypes.bfloat16)
    return np.concatenate([head, head, tail, tail], axis=0)


def in_hbm(*arrays):
    return tuple(pltpu.with_memory_space_constraint(a, pltpu.HBM) for a in arrays)


def head_tail(value):
    head = value.astype(BF16)
    return head, (value - head.astype(F32)).astype(BF16)


UNIT_US, HOP_US, BANDS_US = 2.85, 3.0, 30.0
FOLD_US, REMOVE_US, REMOVE_FOR_US = 20.0, 24.0, 28.0
AHEAD = 0.9
SIZE = {"E": 1.0, "D": 1.0, "H": 0.5, "C": 0.25, "Q": 0.125}
QUARTERED = (1, 3)


def plan_messages():
    out = []
    band = lambda q: [("E", 0, q)] + [("D", q, k) for k in range(3)] + [("H", q), ("C", q)]
    add = lambda link, key, there, half=None, after=None: out.append((link, key, there, half, after or (there,)))
    for link, near in (("ym", 3), ("yp", 1)):
        for unit in band(0) + band(1) + [("E", dz, 1) for dz in (1, 2, 3)]:
            add(link, (0, near, unit), (0, 0, unit))
    for link, near, q, dz, half in (("ym", 3, 0, 1, 0), ("yp", 1, 1, 3, 1)):
        for unit in band(q) + [("E", dz, 1)]:
            add(link, (0, 2, unit), (0, near, unit))
        add(link, (0, 2, ("E", 2, 1)), (0, near, ("E", 2, 1)), half)
    for dy in range(4):
        for own, other in zip(band(0), band(1)):
            if own[0] == "C":
                add("xc", (1, dy, own), (0, dy, other))
                add("xc", (1, dy, other), (0, dy, own))
            elif own[0] == "H" and dy in QUARTERED:
                add("xc", (1, dy, ("Q", 0, 0)), (0, dy, ("Q", 0, 1)), None, ((0, dy, own), (0, dy, other)))
                add("xi", (1, dy, ("Q", 0, 1)), (1, dy, ("Q", 0, 0)))
            else:
                add("xc", (1, dy, own), (0, dy, other))
                add("xi", (1, dy, other), (1, dy, own))
    for link, dz, q, half in (("zm", 3, 0, 0), ("zp", 1, 1, 1)):
        for dy in (1, 2, 3):
            add(link, (0, dy, ("E", dz, 0)), (0, dy, ("E", 0, 0)))
            add(link, (0, dy, ("E", 2, 0)), (0, dy, ("E", dz, 0)), half)
        for dy in range(4):
            for kind in ("E", "Q") if dy in QUARTERED else ("E",):
                for each in (0, 1):
                    add(link, (1, dy, (kind, dz, each)), (1, dy, (kind, 0, each)))
                add(link, (1, dy, (kind, 2, q)), (1, dy, (kind, dz, q)))
    return out


def plan():
    messages = plan_messages()
    users = {}
    for index, message in enumerate(messages):
        for source in message[4]:
            users.setdefault(source, []).append(index)
    cost = [SIZE[m[1][2][0]] * (0.5 if m[3] is not None else 1.0) * UNIT_US for m in messages]
    known = {}

    def tail(index):
        if index not in known:
            after = [tail(user) for user in users.get(messages[index][1], [])]
            known[index] = cost[index] + HOP_US + max(after + [0.0])
        return known[index]

    here = {}
    for message in messages:
        for source in message[4]:
            if source[:2] == (0, 0):
                here[source] = BANDS_US if source[2][0] == "C" else 0.0
    free = dict.fromkeys(("ym", "yp", "xc", "xi", "zm", "zp"), 0.0)
    left = list(range(len(messages)))
    steps = 3 * (ENTRIES // STEP)
    events = [(FOLD_US * (i + 0.5) / steps, 2, i) for i in range(steps)]
    events += [(FOLD_US + 0.1, 2, steps), (BANDS_US - 0.5, 2, steps + 1)]
    events += [(REMOVE_US + REMOVE_FOR_US * (i + 0.5) / steps, 2, steps + 2 + i) for i in range(steps)]
    while left:
        best = None
        for link in free:
            ready = []
            for i in left:
                if messages[i][0] == link and all(source in here for source in messages[i][4]):
                    at = max(here[source] for source in messages[i][4])
                    ready.append((max(free[link], at), -tail(i), i, at))
            if ready:
                first = min(ready)[0]
                pick = min((r for r in ready if r[0] <= first), key=lambda r: r[1:])
                if best is None or pick[0] < best[0]:
                    best = (pick[0], link, pick[2], pick[3])
        begin, link, index, at = best
        left.remove(index)
        free[link] = begin + cost[index]
        key = messages[index][1]
        arrive = free[link] + HOP_US
        events.append((max(at + 0.01, begin - AHEAD * UNIT_US), 1, index))
        events.append((arrive, 0, index))
        here[key] = max(here.get(key, 0.0), arrive)
    return messages, sorted(events)


def spread_kernel(
    gate_m, up_m, down_m, gate_g, up_g, down_g, gate_w, up_w, down_w, transform_in,
    gate_n, up_n, down_n, early, late, coefs,
    m0, m1, m2, g0, g1, g2, w0, w1, w2, transform, packed, rows, totals, lows, bands,
    peers, mine, loaded, stored, received, own, band_sent, band_received, sent, sent_c, side_sent, side_sent_c,
    side_received, side_received_c,
):
    loads = [
        pltpu.make_async_copy(a, b, loaded.at[i])
        for i, (a, b) in enumerate(
            zip(
                (gate_w, up_w, down_w, gate_m, up_m, down_m, gate_g, up_g, down_g, transform_in),
                (w0, w1, w2, m0, m1, m2, g0, g1, g2, transform),
            )
        )
    ]
    for load in loads:
        load.start()
    stores = [
        pltpu.make_async_copy(a, b, stored.at[i])
        for i, (a, b) in enumerate(((m0, gate_n), (m1, up_n), (m2, down_n)))
    ]
    replica, shard = lax.axis_index("replica"), lax.axis_index("fsdp")
    z, lo = lax.div(replica, 2), lax.rem(replica, 2)
    hi, y, core = lax.div(shard, 8), lax.rem(lax.div(shard, 2), 4), lax.rem(shard, 2)
    device = lambda z, lo, hi, y, core: (2 * z + lo, 8 * hi + 2 * y + core)
    turn = lambda at, by: lax.rem(at + by, 4)
    target = {
        "ym": device(z, lo, hi, turn(y, 1), core),
        "yp": device(z, lo, hi, turn(y, 3), core),
        "xc": device(z, 1 - lo, 1 - hi, y, core),
        "xi": device(z, 1 - lo, hi, y, core),
        "zm": device(turn(z, 1), lo, hi, y, core),
        "zp": device(turn(z, 3), lo, hi, y, core),
    }
    sibling = device(z, lo, hi, y, 1 - core)
    fellows = [
        device(turn(z, dz), lo if same else 1 - lo, hi, y, core)
        for dz in range(4)
        for same in (True, False)
        if not (dz == 0 and same)
    ]

    barrier = pltpu.get_barrier_semaphore()
    partners = [target["ym"], target["yp"], target["xc"], sibling] + fellows
    for partner in partners:
        pl.semaphore_signal(barrier, 1, device_id=partner, device_id_type=MESH)

    chunks = [pl.ds(at, STEP) for at in range(0, ENTRIES, STEP)]

    def lay(block, gate, up, down):
        @pl.when(core == 0)
        def _():
            block[0:108, :] = gate
            block[108:112, :] = down[16:20]
            block[112:220, :] = up
            block[220:224, :] = jnp.zeros_like(down[0:4])
            block[224:240, :] = down[0:16]

        @pl.when(core == 1)
        def _():
            block[0:4, :] = down[0:4]
            block[4:112, :] = gate
            block[112:116, :] = jnp.zeros_like(down[0:4])
            block[116:224, :] = up
            block[224:240, :] = down[4:20]

    for load in loads[:3]:
        load.wait()
    for chunk in chunks:
        lay(rows, *(w[:, chunk].astype(F32) for w in (w0, w1, w2)))
        packed[:, chunk] = rows[...].astype(BF16)
    pl.semaphore_wait(barrier, len(partners))

    groups = ENTRIES // 128
    windows = ((m0, g0, 0, 108), (m1, g1, 112, 108), (m2, g2, 224, 20))

    def accumulate(window, chunk):
        momentum, gradient, at, tiles = windows[window]
        if chunk == 0:
            loads[3 + window].wait()
            loads[6 + window].wait()
            if window == 0:
                loads[9].wait()
        pieces = []
        for group in range(chunk * STEP // 128, (chunk + 1) * STEP // 128):
            line = pl.ds(group, tiles, stride=groups)
            piece = 0.999 * momentum[line, :] + gradient[0, :, pl.ds(128 * group, 128)].astype(F32)
            momentum[line, :] = piece
            pieces.append(piece)
        total = None
        for part in head_tail(jnp.concatenate(pieces, axis=1)):
            product = lax.dot_general(
                part,
                transform[COEFS : 3 * COEFS, chunks[chunk]],
                (((1,), (1,)), ((), ())),
                preferred_element_type=F32,
            )
            total = product if total is None else total + product
        spot = pl.ds(at, tiles)
        totals[spot, :] = total if chunk == 0 else totals[spot, :] + total

    def finish_bands():
        both = []
        for _, _, at, tiles in windows:
            total = totals[pl.ds(at, tiles), :]
            both.append(jnp.concatenate(head_tail(total[:, :COEFS] + total[:, COEFS:]), axis=1).astype(F32))
            totals[pl.ds(at, tiles), :] = both[-1]
        lay(lows, *both)
        lows[ROWS:BAND_ROWS, :] = jnp.zeros((BAND_ROWS - ROWS, 2 * COEFS), F32)
        bands[...] = lows[...].astype(BF16)
        for fellow in fellows:
            remote(bands, peers.at[replica], band_sent, band_received, fellow).start()

    def remove(window, chunk):
        momentum, _, at, tiles = windows[window]
        both = totals[pl.ds(at, tiles), :].astype(BF16)
        twice = jnp.concatenate([both, both], axis=1)
        removed = jnp.dot(twice, transform[:, chunks[chunk]], preferred_element_type=F32)
        for part in range(STEP // 128):
            line = pl.ds(chunk * STEP // 128 + part, tiles, stride=groups)
            momentum[line, :] = momentum[line, :] - removed[:, 128 * part : 128 * (part + 1)]
        if chunk == len(chunks) - 1:
            stores[window].start()

    def remote(source, dest, send, receive, to):
        return pltpu.make_async_remote_copy(
            src_ref=source, dst_ref=dest, send_sem=send, recv_sem=receive, device_id=to, device_id_type=MESH
        )

    block_at = {
        (dx, dy): 8 * (hi if dx == 0 else 1 - hi) + 2 * turn(y, dy) + core for dx in range(2) for dy in range(4)
    }
    parity = (lo, 1 - lo)

    def place(array_rows, key, half):
        kind = key[0]
        columns = slice(None) if half is None else pl.ds(half * (ENTRIES // 2), ENTRIES // 2)
        if kind == "E":
            start = 32 * turn(z, key[1]) + 16 * parity[key[2]]
        elif kind == "D":
            start = EARLY + 48 * parity[key[1]] + 16 * key[2]
        elif kind == "H":
            start = 224
            columns = pl.ds(pl.multiple_of((ENTRIES // 2) * parity[key[1]], 128), ENTRIES // 2)
        elif kind == "Q":
            start = 224
            columns = pl.ds(pl.multiple_of(1024 * turn(z, key[1]) + 512 * parity[key[2]], 128), 512)
        else:
            return pl.ds(pl.multiple_of(128 * parity[key[1]], 16), 128), slice(None)
        return (pl.ds(start if isinstance(start, int) else pl.multiple_of(start, 16), 16), columns)

    part = lambda unit: early if unit[0] == "E" else late
    rows_in = lambda unit, rows: rows if unit[0] == "E" else pl.ds(rows.start - EARLY, rows.size)

    def refs(key, half):
        dx, dy, unit = key
        rows, columns = place(None, unit, half)
        block = block_at[(dx, dy)]
        if unit[0] == "C":
            here = coefs.at[block, rows, columns]
            return (mine.at[rows, columns] if (dx, dy) == (0, 0) else here), here
        if (dx, dy) == (0, 0):
            return packed.at[rows, columns], part(unit).at[block, rows_in(unit, rows), columns]
        here = part(unit).at[block, rows_in(unit, rows), columns]
        return here, here

    messages, events = plan()
    slices = [functools.partial(accumulate, w, c) for w in range(3) for c in range(len(chunks))]
    slices += [finish_bands, lambda: average()]
    slices += [functools.partial(remove, w, c) for w in range(3) for c in range(len(chunks))]
    me = block_at[(0, 0)]
    halves = ((packed.at[0:EARLY], early.at[me]), (packed.at[EARLY:ROWS], late.at[me]))
    own_copies = [pltpu.make_async_copy(a, b, own.at[i]) for i, (a, b) in enumerate(halves)]
    own_coefs = pltpu.make_async_copy(mine, coefs.at[me], own.at[2])

    def send(index):
        link, key, key_there, half, _ = messages[index]
        source, dest = refs(key_there, half)
        is_coefs = key[2][0] == "C"
        which = sent_c if is_coefs else sent.at[int(key[2][0] != "E")]
        remote(source, dest, which, received.at[index], target[link]).start()

    def take(index):
        link, key, _, columns, _ = messages[index]
        _, dest = refs(key, columns)
        is_coefs = key[2][0] == "C"
        remote(dest, dest, sent_c, received.at[index], target[link]).wait_recv()
        half = int(key[2][0] != "E")
        remote(
            dest,
            dest,
            side_sent_c if is_coefs else side_sent.at[half],
            side_received_c if is_coefs else side_received.at[half],
            sibling,
        ).start()

    def average():
        peers[replica] = bands[...]
        remote(peers.at[0:7], peers.at[0:7], band_sent, band_received, sibling).wait_recv()
        total = peers[0].astype(F32)
        for each in range(1, 8):
            total = total + peers[each].astype(F32)
        averaged = (total[:, :COEFS] + total[:, COEFS:]) / 8.0
        square = jnp.sum(averaged * averaged, axis=1, keepdims=True) / ENTRIES
        head, tail = head_tail(-0.5 * averaged / jnp.sqrt(square + 1e-06))
        mine[...] = jnp.concatenate([head, tail], axis=1)
        own_coefs.start()
        remote(mine, coefs.at[me], side_sent_c, side_received_c, sibling).start()

    first = True
    for when, kind, index in events:
        if kind == 1:
            send(index)
            continue
        if first:
            for copy in own_copies:
                copy.start()
            for i, (source, dest) in enumerate(halves):
                remote(source, dest, side_sent.at[i], side_received.at[i], sibling).start()
            first = False
        if kind == 2:
            slices[index]()
        else:
            take(index)

    for copy in own_copies:
        copy.wait()
    own_coefs.wait()
    for store in stores:
        store.wait()
    remote(peers.at[0:7], peers.at[0:7], band_sent, band_received, sibling).wait_send()
    for i, each in enumerate((early, late)):
        remote(each.at[0:7], each.at[0:7], sent.at[i], side_received.at[i], sibling).wait_send()
    remote(coefs.at[0:7], coefs.at[0:7], sent_c, side_received_c, sibling).wait_send()
    for i, each in enumerate((early, late)):
        remote(each.at[0:8], each.at[0:8], side_sent.at[i], side_received.at[i], sibling).wait()
    remote(coefs.at[0:8], coefs.at[0:8], side_sent_c, side_received_c, sibling).wait()


def spread(arrays, transform):
    dma = pltpu.SemaphoreType.DMA
    lines = [a.reshape(-1, 128) for a in arrays[:3]]
    here = lambda a: pltpu.VMEM(a.shape, a.dtype)
    band = pltpu.VMEM((BAND_ROWS, 2 * COEFS), BF16)
    return pl.pallas_call(
        spread_kernel,
        name="spread",
        out_shape=tuple(jax.ShapeDtypeStruct(a.shape, F32) for a in lines)
        + (
            jax.ShapeDtypeStruct((16, EARLY, ENTRIES), BF16),
            jax.ShapeDtypeStruct((16, ROWS - EARLY, ENTRIES), BF16),
            jax.ShapeDtypeStruct((16, BAND_ROWS, 2 * COEFS), BF16),
        ),
        in_specs=[ANY] * 10,
        out_specs=(ANY,) * 6,
        scratch_shapes=[here(a) for a in (*lines, *arrays[3:], transform)]
        + [
            pltpu.VMEM((ROWS, ENTRIES), BF16),
            pltpu.VMEM((ROWS, STEP), F32),
            pltpu.VMEM((BAND_ROWS, 2 * COEFS), F32),
            pltpu.VMEM((BAND_ROWS, 2 * COEFS), F32),
            band,
            pltpu.VMEM((8, BAND_ROWS, 2 * COEFS), BF16),
            band,
            dma((10,)),
            dma((3,)),
            dma((len(plan_messages()),)),
            dma((3,)),
        ]
        + [dma] * 2
        + [dma((2,)), dma, dma((2,)), dma, dma((2,)), dma],
        compiler_params=pltpu.CompilerParams(
            collective_id=0, has_side_effects=True, vmem_limit_bytes=16 * 2**20
        ),
    )(*in_hbm(*lines, *arrays[3:], transform))


QUAD = 4
WIDTH = 2048


def refresh_kernel(
    early, late, coefs, transform, gate_m, up_m, down_m, gate, up, down, gate_n, up_n, down_n
):
    gate_n[...] = gate_m[...]
    up_n[...] = up_m[...]
    down_n[...] = down_m[...]
    low_half = lax.broadcasted_iota(jnp.int32, (8, 256), 0) < 4
    first, left = QUAD * pl.program_id(0), WIDTH * pl.program_id(1)
    for at in range(0, WIDTH, 256):
        chunk = pl.ds(at, 256)
        column = pl.ds(pl.multiple_of(left + at, 256), 256)
        gates, ups, downs = [], [], []

        def renewed(each):
            both = coefs[first + each, 0:ROWS, :]
            twice = jnp.concatenate([both, both], axis=1)
            update = jnp.dot(twice, transform[:, chunk], preferred_element_type=F32)
            return (1.0 - 0.5 * 0.1) * jnp.concatenate(
                [early[first + each, :, column].astype(F32), late[first + each, :, column].astype(F32)], axis=0
            ) + update

        for pair in range(QUAD // 2):
            even, odd = renewed(2 * pair), renewed(2 * pair + 1)
            join = lambda a, b: jnp.where(low_half, a, b)
            gates += [even[0:104], join(even[104:112], odd[0:8]), odd[8:112]]
            ups += [even[112:216], join(even[216:224], odd[112:120]), odd[120:224]]
            downs += [
                even[224:240],
                join(pltpu.roll(even[104:112], 4, 0), pltpu.roll(odd[0:8], 4, 0)),
                odd[224:240],
            ]
        gate[:, chunk] = jnp.concatenate(gates, axis=0).astype(BF16)
        up[:, chunk] = jnp.concatenate(ups, axis=0).astype(BF16)
        down[:, chunk] = jnp.concatenate(downs, axis=0).astype(BF16)


def refresh(early, late, coefs, transform, moments):
    whole = lambda rows: jax.ShapeDtypeStruct((16 * rows, ENTRIES), BF16)
    out = lambda rows: pl.BlockSpec((QUAD * rows, WIDTH), lambda g, c: (g, c))
    steps = (16 // QUAD) * (ENTRIES // WIDTH)
    moment_specs = tuple(
        pl.BlockSpec((a.shape[0] // steps, 128), lambda g, c: (g * (ENTRIES // WIDTH) + c, 0)) for a in moments
    )
    return pl.pallas_call(
        refresh_kernel,
        name="refresh",
        grid=(16 // QUAD, ENTRIES // WIDTH),
        out_shape=(whole(108), whole(108), whole(20))
        + tuple(jax.ShapeDtypeStruct(a.shape, F32) for a in moments),
        in_specs=[
            VMEM,
            VMEM,
            VMEM,
            pl.BlockSpec((4 * COEFS, WIDTH), lambda g, c: (0, c)),
            *moment_specs,
        ],
        out_specs=(out(108), out(108), out(20)) + moment_specs,
        compiler_params=pltpu.CompilerParams(vmem_limit_bytes=14 * 2**20),
    )(early, late, coefs, transform, *moments)


def on_device(*arrays):
    transform = jnp.asarray(split_transform())
    *moments, early, late, coefs = spread(arrays, transform)
    *whole, gate_next, up_next, down_next = refresh(early, late, coefs, transform, moments)
    following = [a.reshape(b.shape) for a, b in zip((gate_next, up_next, down_next), arrays)]
    return (*following, *whole)


def solution(mesh):
    by_replica, by_shard = P("replica", "fsdp", None), P("fsdp", None)
    return jax.shard_map(
        on_device,
        mesh=mesh,
        in_specs=(by_replica,) * 6 + (by_shard,) * 3,
        out_specs=(by_replica,) * 3 + (P(),) * 3,
        check_vma=False,
    )
```

```python
import functools

import jax
import jax.numpy as jnp
import ml_dtypes
import numpy as np
from jax import lax
from jax.experimental import pallas as pl
from jax.experimental.pallas import tpu as pltpu
from jax.sharding import PartitionSpec as P

TILE = 64
BAND = 8
COEFS = BAND * BAND
ENTRIES = TILE * TILE
F32 = jnp.float32
BF16 = jnp.bfloat16
MESH = pl.DeviceIdType.MESH
ANY = pl.BlockSpec(memory_space=pl.ANY)
VMEM = pl.BlockSpec(memory_space=pltpu.VMEM)

ROWS = 240
BAND_ROWS = 256
EARLY = 128
STEP = 512


def split_transform():
    freq = np.arange(BAND, dtype=np.float64)[:, None]
    position = np.arange(TILE, dtype=np.float64)[None, :]
    cosines = np.sqrt(2.0 / TILE) * np.cos(np.pi * (2.0 * position + 1.0) * freq / (2.0 * TILE))
    cosines[0] *= np.sqrt(0.5)
    product = (cosines[:, None, :, None] * cosines[None, :, None, :]).reshape(COEFS, ENTRIES)
    head = product.astype(np.float32).astype(ml_dtypes.bfloat16)
    tail = (product - head.astype(np.float64)).astype(np.float32).astype(ml_dtypes.bfloat16)
    return np.concatenate([head, head, tail, tail], axis=0)


def in_hbm(*arrays):
    return tuple(pltpu.with_memory_space_constraint(a, pltpu.HBM) for a in arrays)


def head_tail(value):
    head = value.astype(BF16)
    return head, (value - head.astype(F32)).astype(BF16)


UNIT_US, HOP_US, BANDS_US = 2.85, 3.0, 30.0
FOLD_US, REMOVE_US, REMOVE_FOR_US = 20.0, 24.0, 28.0
AHEAD = 0.9
SIZE = {"E": 1.0, "D": 1.0, "H": 0.5, "C": 0.25, "Q": 0.125}
QUARTERED = (1, 3)


def plan_messages():
    out = []
    band = lambda q: [("E", 0, q)] + [("D", q, k) for k in range(3)] + [("H", q), ("C", q)]
    add = lambda link, key, there, half=None, after=None: out.append((link, key, there, half, after or (there,)))
    for link, near in (("ym", 3), ("yp", 1)):
        for unit in band(0) + band(1) + [("E", dz, 1) for dz in (1, 2, 3)]:
            add(link, (0, near, unit), (0, 0, unit))
    for link, near, q, dz, half in (("ym", 3, 0, 1, 0), ("yp", 1, 1, 3, 1)):
        for unit in band(q) + [("E", dz, 1)]:
            add(link, (0, 2, unit), (0, near, unit))
        add(link, (0, 2, ("E", 2, 1)), (0, near, ("E", 2, 1)), half)
    for dy in range(4):
        for own, other in zip(band(0), band(1)):
            if own[0] == "C":
                add("xc", (1, dy, own), (0, dy, other))
                add("xc", (1, dy, other), (0, dy, own))
            elif own[0] == "H" and dy in QUARTERED:
                add("xc", (1, dy, ("Q", 0, 0)), (0, dy, ("Q", 0, 1)), None, ((0, dy, own), (0, dy, other)))
                add("xi", (1, dy, ("Q", 0, 1)), (1, dy, ("Q", 0, 0)))
            else:
                add("xc", (1, dy, own), (0, dy, other))
                add("xi", (1, dy, other), (1, dy, own))
    for link, dz, q, half in (("zm", 3, 0, 0), ("zp", 1, 1, 1)):
        for dy in (1, 2, 3):
            add(link, (0, dy, ("E", dz, 0)), (0, dy, ("E", 0, 0)))
            add(link, (0, dy, ("E", 2, 0)), (0, dy, ("E", dz, 0)), half)
        for dy in range(4):
            for kind in ("E", "Q") if dy in QUARTERED else ("E",):
                for each in (0, 1):
                    add(link, (1, dy, (kind, dz, each)), (1, dy, (kind, 0, each)))
                add(link, (1, dy, (kind, 2, q)), (1, dy, (kind, dz, q)))
    return out


def plan():
    messages = plan_messages()
    users = {}
    for index, message in enumerate(messages):
        for source in message[4]:
            users.setdefault(source, []).append(index)
    cost = [SIZE[m[1][2][0]] * (0.5 if m[3] is not None else 1.0) * UNIT_US for m in messages]
    known = {}

    def tail(index):
        if index not in known:
            after = [tail(user) for user in users.get(messages[index][1], [])]
            known[index] = cost[index] + HOP_US + max(after + [0.0])
        return known[index]

    here = {}
    for message in messages:
        for source in message[4]:
            if source[:2] == (0, 0):
                here[source] = BANDS_US if source[2][0] == "C" else 0.0
    free = dict.fromkeys(("ym", "yp", "xc", "xi", "zm", "zp"), 0.0)
    left = list(range(len(messages)))
    steps = 3 * (ENTRIES // STEP)
    events = [(FOLD_US * (i + 0.5) / steps, 2, i) for i in range(steps)]
    events += [(FOLD_US + 0.1, 2, steps), (BANDS_US - 0.5, 2, steps + 1)]
    events += [(REMOVE_US + REMOVE_FOR_US * (i + 0.5) / steps, 2, steps + 2 + i) for i in range(steps)]
    while left:
        best = None
        for link in free:
            ready = []
            for i in left:
                if messages[i][0] == link and all(source in here for source in messages[i][4]):
                    at = max(here[source] for source in messages[i][4])
                    ready.append((max(free[link], at), -tail(i), i, at))
            if ready:
                first = min(ready)[0]
                pick = min((r for r in ready if r[0] <= first), key=lambda r: r[1:])
                if best is None or pick[0] < best[0]:
                    best = (pick[0], link, pick[2], pick[3])
        begin, link, index, at = best
        left.remove(index)
        free[link] = begin + cost[index]
        key = messages[index][1]
        arrive = free[link] + HOP_US
        events.append((max(at + 0.01, begin - AHEAD * UNIT_US), 1, index))
        events.append((arrive, 0, index))
        here[key] = max(here.get(key, 0.0), arrive)
    return messages, sorted(events)


def spread_kernel(
    gate_m, up_m, down_m, gate_g, up_g, down_g, gate_w, up_w, down_w, transform_in,
    gate_n, up_n, down_n, early, late, coefs,
    m0, m1, m2, g0, g1, g2, w0, w1, w2, transform, packed, rows, totals, lows, bands,
    peers, mine, loaded, stored, received, own, band_sent, band_received, sent, sent_c, side_sent, side_sent_c,
    side_received, side_received_c,
):
    loads = [
        pltpu.make_async_copy(a, b, loaded.at[i])
        for i, (a, b) in enumerate(
            zip(
                (gate_w, up_w, down_w, gate_m, up_m, down_m, gate_g, up_g, down_g, transform_in),
                (w0, w1, w2, m0, m1, m2, g0, g1, g2, transform),
            )
        )
    ]
    for load in loads:
        load.start()
    stores = [
        pltpu.make_async_copy(a, b, stored.at[i])
        for i, (a, b) in enumerate(((m0, gate_n), (m1, up_n), (m2, down_n)))
    ]
    replica, shard = lax.axis_index("replica"), lax.axis_index("fsdp")
    z, lo = lax.div(replica, 2), lax.rem(replica, 2)
    hi, y, core = lax.div(shard, 8), lax.rem(lax.div(shard, 2), 4), lax.rem(shard, 2)
    device = lambda z, lo, hi, y, core: (2 * z + lo, 8 * hi + 2 * y + core)
    turn = lambda at, by: lax.rem(at + by, 4)
    target = {
        "ym": device(z, lo, hi, turn(y, 1), core),
        "yp": device(z, lo, hi, turn(y, 3), core),
        "xc": device(z, 1 - lo, 1 - hi, y, core),
        "xi": device(z, 1 - lo, hi, y, core),
        "zm": device(turn(z, 1), lo, hi, y, core),
        "zp": device(turn(z, 3), lo, hi, y, core),
    }
    sibling = device(z, lo, hi, y, 1 - core)
    fellows = [
        device(turn(z, dz), lo if same else 1 - lo, hi, y, core)
        for dz in range(4)
        for same in (True, False)
        if not (dz == 0 and same)
    ]

    barrier = pltpu.get_barrier_semaphore()
    partners = [target["ym"], target["yp"], target["xc"], sibling] + fellows
    for partner in partners:
        pl.semaphore_signal(barrier, 1, device_id=partner, device_id_type=MESH)

    chunks = [pl.ds(at, STEP) for at in range(0, ENTRIES, STEP)]

    def lay(block, gate, up, down):
        @pl.when(core == 0)
        def _():
            block[0:108, :] = gate
            block[108:112, :] = down[16:20]
            block[112:220, :] = up
            block[220:224, :] = jnp.zeros_like(down[0:4])
            block[224:240, :] = down[0:16]

        @pl.when(core == 1)
        def _():
            block[0:4, :] = down[0:4]
            block[4:112, :] = gate
            block[112:116, :] = jnp.zeros_like(down[0:4])
            block[116:224, :] = up
            block[224:240, :] = down[4:20]

    for load in loads[:3]:
        load.wait()
    for chunk in chunks:
        lay(rows, *(w[:, chunk].astype(F32) for w in (w0, w1, w2)))
        packed[:, chunk] = rows[...].astype(BF16)
    pl.semaphore_wait(barrier, len(partners))

    groups = ENTRIES // 128
    windows = ((m0, g0, 0, 108), (m1, g1, 112, 108), (m2, g2, 224, 20))

    def accumulate(window, chunk):
        momentum, gradient, at, tiles = windows[window]
        if chunk == 0:
            loads[3 + window].wait()
            loads[6 + window].wait()
            if window == 0:
                loads[9].wait()
        pieces = []
        for group in range(chunk * STEP // 128, (chunk + 1) * STEP // 128):
            line = pl.ds(group, tiles, stride=groups)
            piece = 0.999 * momentum[line, :] + gradient[0, :, pl.ds(128 * group, 128)].astype(F32)
            momentum[line, :] = piece
            pieces.append(piece)
        total = None
        for part in head_tail(jnp.concatenate(pieces, axis=1)):
            product = lax.dot_general(
                part,
                transform[COEFS : 3 * COEFS, chunks[chunk]],
                (((1,), (1,)), ((), ())),
                preferred_element_type=F32,
            )
            total = product if total is None else total + product
        spot = pl.ds(at, tiles)
        totals[spot, :] = total if chunk == 0 else totals[spot, :] + total

    def finish_bands():
        both = []
        for _, _, at, tiles in windows:
            total = totals[pl.ds(at, tiles), :]
            both.append(jnp.concatenate(head_tail(total[:, :COEFS] + total[:, COEFS:]), axis=1).astype(F32))
            totals[pl.ds(at, tiles), :] = both[-1]
        lay(lows, *both)
        lows[ROWS:BAND_ROWS, :] = jnp.zeros((BAND_ROWS - ROWS, 2 * COEFS), F32)
        bands[...] = lows[...].astype(BF16)
        for fellow in fellows:
            remote(bands, peers.at[replica], band_sent, band_received, fellow).start()

    def remove(window, chunk):
        momentum, _, at, tiles = windows[window]
        both = totals[pl.ds(at, tiles), :].astype(BF16)
        twice = jnp.concatenate([both, both], axis=1)
        removed = jnp.dot(twice, transform[:, chunks[chunk]], preferred_element_type=F32)
        for part in range(STEP // 128):
            line = pl.ds(chunk * STEP // 128 + part, tiles, stride=groups)
            momentum[line, :] = momentum[line, :] - removed[:, 128 * part : 128 * (part + 1)]
        if chunk == len(chunks) - 1:
            stores[window].start()

    def remote(source, dest, send, receive, to):
        return pltpu.make_async_remote_copy(
            src_ref=source, dst_ref=dest, send_sem=send, recv_sem=receive, device_id=to, device_id_type=MESH
        )

    block_at = {
        (dx, dy): 8 * (hi if dx == 0 else 1 - hi) + 2 * turn(y, dy) + core for dx in range(2) for dy in range(4)
    }
    parity = (lo, 1 - lo)

    def place(array_rows, key, half):
        kind = key[0]
        columns = slice(None) if half is None else pl.ds(half * (ENTRIES // 2), ENTRIES // 2)
        if kind == "E":
            start = 32 * turn(z, key[1]) + 16 * parity[key[2]]
        elif kind == "D":
            start = EARLY + 48 * parity[key[1]] + 16 * key[2]
        elif kind == "H":
            start = 224
            columns = pl.ds(pl.multiple_of((ENTRIES // 2) * parity[key[1]], 128), ENTRIES // 2)
        elif kind == "Q":
            start = 224
            columns = pl.ds(pl.multiple_of(1024 * turn(z, key[1]) + 512 * parity[key[2]], 128), 512)
        else:
            return pl.ds(pl.multiple_of(128 * parity[key[1]], 16), 128), slice(None)
        return (pl.ds(start if isinstance(start, int) else pl.multiple_of(start, 16), 16), columns)

    part = lambda unit: early if unit[0] == "E" else late
    rows_in = lambda unit, rows: rows if unit[0] == "E" else pl.ds(rows.start - EARLY, rows.size)

    def refs(key, half):
        dx, dy, unit = key
        rows, columns = place(None, unit, half)
        block = block_at[(dx, dy)]
        if unit[0] == "C":
            here = coefs.at[block, rows, columns]
            return (mine.at[rows, columns] if (dx, dy) == (0, 0) else here), here
        if (dx, dy) == (0, 0):
            return packed.at[rows, columns], part(unit).at[block, rows_in(unit, rows), columns]
        here = part(unit).at[block, rows_in(unit, rows), columns]
        return here, here

    messages, events = plan()
    slices = [functools.partial(accumulate, w, c) for w in range(3) for c in range(len(chunks))]
    slices += [finish_bands, lambda: average()]
    slices += [functools.partial(remove, w, c) for w in range(3) for c in range(len(chunks))]
    me = block_at[(0, 0)]
    halves = ((packed.at[0:EARLY], early.at[me]), (packed.at[EARLY:ROWS], late.at[me]))
    own_copies = [pltpu.make_async_copy(a, b, own.at[i]) for i, (a, b) in enumerate(halves)]
    own_coefs = pltpu.make_async_copy(mine, coefs.at[me], own.at[2])

    def send(index):
        link, key, key_there, half, _ = messages[index]
        source, dest = refs(key_there, half)
        is_coefs = key[2][0] == "C"
        which = sent_c if is_coefs else sent.at[int(key[2][0] != "E")]
        remote(source, dest, which, received.at[index], target[link]).start()

    def take(index):
        link, key, _, columns, _ = messages[index]
        _, dest = refs(key, columns)
        is_coefs = key[2][0] == "C"
        remote(dest, dest, sent_c, received.at[index], target[link]).wait_recv()
        half = int(key[2][0] != "E")
        remote(
            dest,
            dest,
            side_sent_c if is_coefs else side_sent.at[half],
            side_received_c if is_coefs else side_received.at[half],
            sibling,
        ).start()

    def average():
        peers[replica] = bands[...]
        remote(peers.at[0:7], peers.at[0:7], band_sent, band_received, sibling).wait_recv()
        total = peers[0].astype(F32)
        for each in range(1, 8):
            total = total + peers[each].astype(F32)
        averaged = (total[:, :COEFS] + total[:, COEFS:]) / 8.0
        square = jnp.sum(averaged * averaged, axis=1, keepdims=True) / ENTRIES
        head, tail = head_tail(-0.5 * averaged / jnp.sqrt(square + 1e-06))
        mine[...] = jnp.concatenate([head, tail], axis=1)
        own_coefs.start()
        remote(mine, coefs.at[me], side_sent_c, side_received_c, sibling).start()

    first = True
    for when, kind, index in events:
        if kind == 1:
            send(index)
            continue
        if first:
            for copy in own_copies:
                copy.start()
            for i, (source, dest) in enumerate(halves):
                remote(source, dest, side_sent.at[i], side_received.at[i], sibling).start()
            first = False
        if kind == 2:
            slices[index]()
        else:
            take(index)

    for copy in own_copies:
        copy.wait()
    own_coefs.wait()
    for store in stores:
        store.wait()
    remote(peers.at[0:7], peers.at[0:7], band_sent, band_received, sibling).wait_send()
    for i, each in enumerate((early, late)):
        remote(each.at[0:7], each.at[0:7], sent.at[i], side_received.at[i], sibling).wait_send()
    remote(coefs.at[0:7], coefs.at[0:7], sent_c, side_received_c, sibling).wait_send()
    for i, each in enumerate((early, late)):
        remote(each.at[0:8], each.at[0:8], side_sent.at[i], side_received.at[i], sibling).wait()
    remote(coefs.at[0:8], coefs.at[0:8], side_sent_c, side_received_c, sibling).wait()


def spread(arrays, transform):
    dma = pltpu.SemaphoreType.DMA
    lines = [a.reshape(-1, 128) for a in arrays[:3]]
    here = lambda a: pltpu.VMEM(a.shape, a.dtype)
    band = pltpu.VMEM((BAND_ROWS, 2 * COEFS), BF16)
    return pl.pallas_call(
        spread_kernel,
        name="spread",
        out_shape=tuple(jax.ShapeDtypeStruct(a.shape, F32) for a in lines)
        + (
            jax.ShapeDtypeStruct((16, EARLY, ENTRIES), BF16),
            jax.ShapeDtypeStruct((16, ROWS - EARLY, ENTRIES), BF16),
            jax.ShapeDtypeStruct((16, BAND_ROWS, 2 * COEFS), BF16),
        ),
        in_specs=[ANY] * 10,
        out_specs=(ANY,) * 6,
        scratch_shapes=[here(a) for a in (*lines, *arrays[3:], transform)]
        + [
            pltpu.VMEM((ROWS, ENTRIES), BF16),
            pltpu.VMEM((ROWS, STEP), F32),
            pltpu.VMEM((BAND_ROWS, 2 * COEFS), F32),
            pltpu.VMEM((BAND_ROWS, 2 * COEFS), F32),
            band,
            pltpu.VMEM((8, BAND_ROWS, 2 * COEFS), BF16),
            band,
            dma((10,)),
            dma((3,)),
            dma((len(plan_messages()),)),
            dma((3,)),
        ]
        + [dma] * 2
        + [dma((2,)), dma, dma((2,)), dma, dma((2,)), dma],
        compiler_params=pltpu.CompilerParams(
            collective_id=0, has_side_effects=True, vmem_limit_bytes=16 * 2**20
        ),
    )(*in_hbm(*lines, *arrays[3:], transform))


QUAD = 4
WIDTH = 2048


def refresh_kernel(
    early, late, coefs, transform, gate_m, up_m, down_m, gate, up, down, gate_n, up_n, down_n
):
    step = pl.program_id(0) * pl.num_programs(1) + pl.program_id(1)
    for source, dest in ((gate_m, gate_n), (up_m, up_n), (down_m, down_n)):
        lines = dest.shape[0]
        dest[...] = source[pl.ds(pl.multiple_of(step * lines, 8), lines), :]
    low_half = lax.broadcasted_iota(jnp.int32, (8, 256), 0) < 4
    first, left = QUAD * pl.program_id(0), WIDTH * pl.program_id(1)
    for at in range(0, WIDTH, 256):
        chunk = pl.ds(at, 256)
        column = pl.ds(pl.multiple_of(left + at, 256), 256)
        gates, ups, downs = [], [], []

        def renewed(each):
            both = coefs[first + each, 0:ROWS, :]
            twice = jnp.concatenate([both, both], axis=1)
            update = jnp.dot(twice, transform[:, column], preferred_element_type=F32)
            return (1.0 - 0.5 * 0.1) * jnp.concatenate(
                [early[first + each, :, column].astype(F32), late[first + each, :, column].astype(F32)], axis=0
            ) + update

        for pair in range(QUAD // 2):
            even, odd = renewed(2 * pair), renewed(2 * pair + 1)
            join = lambda a, b: jnp.where(low_half, a, b)
            gates += [even[0:104], join(even[104:112], odd[0:8]), odd[8:112]]
            ups += [even[112:216], join(even[216:224], odd[112:120]), odd[120:224]]
            downs += [
                even[224:240],
                join(pltpu.roll(even[104:112], 4, 0), pltpu.roll(odd[0:8], 4, 0)),
                odd[224:240],
            ]
        gate[:, chunk] = jnp.concatenate(gates, axis=0).astype(BF16)
        up[:, chunk] = jnp.concatenate(ups, axis=0).astype(BF16)
        down[:, chunk] = jnp.concatenate(downs, axis=0).astype(BF16)


def refresh(early, late, coefs, transform, moments):
    whole = lambda rows: jax.ShapeDtypeStruct((16 * rows, ENTRIES), BF16)
    out = lambda rows: pl.BlockSpec((QUAD * rows, WIDTH), lambda g, c: (g, c))
    steps = (16 // QUAD) * (ENTRIES // WIDTH)
    moment_specs = tuple(
        pl.BlockSpec((a.shape[0] // steps, 128), lambda g, c: (g * (ENTRIES // WIDTH) + c, 0)) for a in moments
    )
    return pl.pallas_call(
        refresh_kernel,
        name="refresh",
        grid=(16 // QUAD, ENTRIES // WIDTH),
        out_shape=(whole(108), whole(108), whole(20))
        + tuple(jax.ShapeDtypeStruct(a.shape, F32) for a in moments),
        in_specs=[
            VMEM,
            VMEM,
            VMEM,
            VMEM,
            *[VMEM] * len(moments),
        ],
        out_specs=(out(108), out(108), out(20)) + moment_specs,
        compiler_params=pltpu.CompilerParams(vmem_limit_bytes=14 * 2**20),
    )(early, late, coefs, transform, *moments)


def on_device(*arrays):
    transform = jnp.asarray(split_transform())
    *moments, early, late, coefs = spread(arrays, transform)
    *whole, gate_next, up_next, down_next = refresh(early, late, coefs, transform, moments)
    following = [a.reshape(b.shape) for a, b in zip((gate_next, up_next, down_next), arrays)]
    return (*following, *whole)


def solution(mesh):
    by_replica, by_shard = P("replica", "fsdp", None), P("fsdp", None)
    return jax.shard_map(
        on_device,
        mesh=mesh,
        in_specs=(by_replica,) * 6 + (by_shard,) * 3,
        out_specs=(by_replica,) * 3 + (P(),) * 3,
        check_vma=False,
    )
```
